32 devices in a mesh: screen: 4 (over z), depth: 8 (over y, x, core).
Axes of the slice: x: 2, y: 2, z: 4, core: 2. Of those that a mesh axis runs over, the one named last changes fastest.
Arguments:
- density: bfloat16 [64, 64, 512], P('depth', None, 'screen'), as said below
- bin_index: int32 [64, 64, 512], P('depth', None, 'screen'), may hold values from 0 to 255
- transfer: bfloat16 [4, 256], replicated, may hold values from 0.049804688 to 1
- view_side: int32 [512], P('screen'), may hold values 0 or 1
Outputs:
- image: float32 [4, 64, 512], P(None, 'depth', 'screen')
The draws below stay inside these ranges and needn't reach their ends.
Inputs may be any that keep to these rules, and one draw needn't show every extreme that they name: Up to bfloat16 rounding a voxel's density lies between bin_index / 256 and (bin_index + 1) / 256.
All inputs are finite; a program needn't handle non-finite values. No bound on the sum of `view_side` on one device may be relied on, other than what follows from the above.
Results may differ from the reference program's by a relative error of at most 0.0003.
Values may be sent and summed in bfloat16 or wider, within the bound.
A program may use at most 64 MiB of HBM per device.

```python
import jax
import jax.numpy as jnp
from jax import lax

BINS = 256
COL_DEV = 128
COLS = 512
ROWS = 64
DEPTH = 64
N_SCREEN = 4


def bin_field(key):
    return jax.random.randint(jax.random.fold_in(key, 11), (DEPTH, ROWS, COLS), 0, BINS, dtype=jnp.int32)


def draw_bin_index(key, part):
    return bin_field(key)


def draw_density(key, part):
    levels = bin_field(key).astype(jnp.float32)
    fraction = jax.random.uniform(jax.random.fold_in(key, 12), (DEPTH, ROWS, COLS), jnp.float32)
    fraction = fraction * 0.98
    return ((levels + fraction) / BINS).astype(jnp.bfloat16)


def plant(values, own_key, smallest, largest):
    place = [jax.random.randint(jax.random.fold_in(own_key, axis), (), 0, length) for axis, length in enumerate(values.shape)]
    longest = values.shape.index(max(values.shape))
    neighbour = place[:longest] + [(place[longest] + 1) % values.shape[longest]] + place[longest + 1:]
    return values.at[tuple(place)].set(smallest).at[tuple(neighbour)].set(largest)


def setup_inputs(seed: int = 0) -> dict:
    seeds = jax.random.split(jax.random.key(seed), 5)
    density = draw_density(jax.random.fold_in(seeds[4], 71), 0)
    bin_index = draw_bin_index(jax.random.fold_in(seeds[4], 71), 0)
    transfer = jnp.clip(jax.random.uniform(seeds[2], (4, BINS), jnp.float32, 0.049804688, 1.0), 0.049804688, 1.0).astype(jnp.bfloat16)
    view_side = plant((jax.random.randint(seeds[3], (COLS,), 0, 2) < 1).astype(jnp.int32), jax.random.fold_in(seeds[3], 1), 0, 1)
    return dict(density=density, bin_index=bin_index, transfer=transfer, view_side=view_side)


LIGHT_DIRECTION = (0.36, 0.48, 0.8)
AMBIENT = 0.3
DIFFUSE = 0.7
OPTICAL = 4.0

def centred_diff(field, axis):
    length = field.shape[axis] - 4

    def shifted(offset):
        return lax.slice_in_dim(field, 2 + offset, 2 + offset + length, axis=axis)
    return (8.0 * (shifted(1) - shifted(-1)) - (shifted(2) - shifted(-2))) / 12.0

def shading_of(padded):
    field = padded.astype(jnp.float32)
    grad_depth = centred_diff(field[:, 2:-2, 2:-2], 0)
    grad_rows = centred_diff(field[2:-2, :, 2:-2], 1)
    grad_cols = centred_diff(field[2:-2, 2:-2, :], 2)
    light_dot = LIGHT_DIRECTION[0] * grad_cols + LIGHT_DIRECTION[1] * grad_rows + LIGHT_DIRECTION[2] * grad_depth
    squared = grad_cols * grad_cols + grad_rows * grad_rows + grad_depth * grad_depth
    return AMBIENT + DIFFUSE * jnp.abs(light_dot) / jnp.sqrt(squared + 1.0)

def render(padded, bin_block, side_block, transfer):
    shading = shading_of(padded)
    table = transfer.astype(jnp.float32)
    extinction = table[3][bin_block]
    optical = extinction * (OPTICAL / DEPTH)
    opacity = 1.0 - jnp.exp(-optical)
    running = jnp.cumsum(optical, axis=0)
    through = running[-1]
    before = jnp.where(side_block == 0, running - optical, through[None] - running)
    weight = jnp.exp(-before) * opacity * shading
    channels = []
    for channel in range(3):
        emission = table[channel][bin_block]
        channels.append(lax.optimization_barrier(jnp.sum(emission * weight, axis=0)))
    channels.append(1.0 - jnp.exp(-through))
    return jnp.stack(channels, axis=0)

def reference(density, bin_index, transfer, view_side):
    padded_all = jnp.pad(density, 2)

    def column_part(index):
        offset = (index * COL_DEV).astype(jnp.int32)
        padded = lax.dynamic_slice_in_dim(padded_all, offset, COL_DEV + 4, axis=2)
        bin_block = lax.dynamic_slice_in_dim(bin_index, offset, COL_DEV, axis=2)
        side_block = lax.dynamic_slice_in_dim(view_side, offset, COL_DEV, axis=0)
        return render(padded, bin_block, side_block, transfer)
    pieces = lax.map(column_part, jnp.arange(N_SCREEN, dtype=jnp.int32))
    return jnp.transpose(pieces, (1, 2, 0, 3)).reshape(4, ROWS, COLS)
```

```python
import functools

import jax
import jax.numpy as jnp
from jax import lax
from jax.experimental import pallas as pl
from jax.experimental.pallas import tpu as pltpu
from jax.sharding import PartitionSpec as P

LIGHT_DIRECTION = (0.36, 0.48, 0.8)
AMBIENT = 0.3
DIFFUSE = 0.7
OPTICAL = 4.0
UNIT = 4096
MESH = pl.DeviceIdType.MESH
F32 = jnp.float32
BF16 = jnp.bfloat16


def lane_gather(table, lanes):
    return lax.gather(
        table,
        lanes[..., None],
        lax.GatherDimensionNumbers(
            offset_dims=(),
            collapsed_slice_dims=(1,),
            start_index_map=(1,),
            operand_batching_dims=(0,),
            start_indices_batching_dims=(0,),
        ),
        slice_sizes=(1, 1),
        mode=lax.GatherScatterMode.PROMISE_IN_BOUNDS,
    )


def stencil(distance):
    one = jnp.where(distance == 1, 8.0, jnp.where(distance == -1, -8.0, 0.0))
    two = jnp.where(distance == 2, -1.0, jnp.where(distance == -2, 1.0, 0.0))
    return (one + two).astype(BF16)


def iota(shape, axis):
    return lax.broadcasted_iota(jnp.int32, shape, axis)


def matmul(a, b, dims=((1,), (0,))):
    return lax.dot_general(a, b, (dims, ((), ())), preferred_element_type=F32)


def render_kernel(
    count, screens,
    density_hbm, bins_hbm, table_ref, side_ref, image_ref,
    dens, bins, layer_halo, edge, edge_halo, field, grad_r, grad_c, shade_in,
    send, land,
    in_sem, halo_send, halo_recv, part_send, part_recv,
):
    layers, rows, cols = density_hbm.shape
    block = rows // count
    me = lax.axis_index("depth")
    col = lax.axis_index("screen")
    has_prev, has_next = me > 0, me < count - 1
    has_left, has_right = col > 0, col < screens - 1
    powers = count & (count - 1) == 0

    def partner(k):
        return me ^ k if powers else lax.rem(me + k, count)

    load_dens = pltpu.make_async_copy(density_hbm, dens, in_sem.at[0])
    load_bins = pltpu.make_async_copy(bins_hbm, bins, in_sem.at[1])
    load_dens.start()
    load_bins.start()

    barrier = pltpu.get_barrier_semaphore()
    for k in range(1, count):
        pl.semaphore_signal(barrier, inc=1, device_id={"depth": partner(k)}, device_id_type=MESH)

    @pl.when(has_left)
    def _():
        pl.semaphore_signal(barrier, inc=1, device_id={"screen": col - 1}, device_id_type=MESH)

    @pl.when(has_right)
    def _():
        pl.semaphore_signal(barrier, inc=1, device_id={"screen": col + 1}, device_id_type=MESH)

    zeros_layer = jnp.zeros((2, rows, cols), BF16)
    zeros_edge = jnp.zeros((16, layers * rows), BF16)

    @pl.when(jnp.logical_not(has_prev))
    def _():
        layer_halo[0] = zeros_layer

    @pl.when(jnp.logical_not(has_next))
    def _():
        layer_halo[1] = zeros_layer

    @pl.when(jnp.logical_not(has_left))
    def _():
        edge_halo[pl.ds(0, 16)] = zeros_edge

    @pl.when(jnp.logical_not(has_right))
    def _():
        edge_halo[pl.ds(16, 16)] = zeros_edge

    greeted = count - 1 + has_left.astype(jnp.int32) + has_right.astype(jnp.int32)
    pl.semaphore_wait(barrier, greeted)

    def remote(src, dst, send_sem, recv_sem, target):
        return pltpu.make_async_remote_copy(
            src_ref=src, dst_ref=dst, send_sem=send_sem, recv_sem=recv_sem,
            device_id=target, device_id_type=MESH,
        )

    halos = (
        (has_next, has_prev, remote(
            density_hbm.at[pl.ds(layers - 2, 2)], layer_halo.at[0],
            halo_send.at[0], halo_recv.at[0], {"depth": me + 1})),
        (has_prev, has_next, remote(
            density_hbm.at[pl.ds(0, 2)], layer_halo.at[1],
            halo_send.at[1], halo_recv.at[1], {"depth": me - 1})),
        (has_right, has_left, remote(
            edge, edge_halo.at[pl.ds(0, 16)],
            halo_send.at[2], halo_recv.at[2], {"screen": col + 1})),
        (has_left, has_right, remote(
            edge, edge_halo.at[pl.ds(16, 16)],
            halo_send.at[3], halo_recv.at[3], {"screen": col - 1})),
    )
    for sends, _, copy in halos[:2]:
        pl.when(sends)(copy.start)

    load_dens.wait()
    flat = dens[...].reshape(layers * rows, cols)
    slot = iota((16, cols), 0)
    wanted = jnp.where(slot < 2, slot, jnp.where(slot < 4, cols - 4 + slot, -1))
    pick = (iota((16, cols), 1) == wanted).astype(F32).astype(BF16)
    edge[...] = matmul(pick, flat, ((1,), (1,))).astype(BF16)
    for sends, _, copy in halos[2:]:
        pl.when(sends)(copy.start)

    band_c = stencil(iota((cols, cols), 0) - iota((cols, cols), 1))
    band_r = stencil(iota((rows, rows), 1) - iota((rows, rows), 0))
    grad_c[...] = matmul(flat, band_c).reshape(layers, rows, cols)
    for z in range(layers):
        grad_r[z] = matmul(band_r, dens[z])
    field[pl.ds(2, layers)] = dens[...].astype(F32)

    load_bins.wait()
    units = (table_ref[...].astype(F32) * UNIT).astype(jnp.int32)
    pairs = (units[0:1] | (units[1:2] << 16), units[2:3] | (units[3:4] << 16))
    half = units.shape[1] // 2
    lows = [jnp.broadcast_to(p[:, :half], (block, half)) for p in pairs]
    highs = [jnp.broadcast_to(p[:, half:], (block, half)) for p in pairs]
    near = jnp.broadcast_to(side_ref[...] == 0, (block, cols))
    optical_scale = -OPTICAL / (layers * count) / UNIT

    def lookup_block(b, carry):
        r0 = pl.multiple_of(b * block, block)
        clear, reds, greens, blues = [], [], [], []
        for z in range(layers):
            index = bins[z, pl.ds(r0, block), :]
            lane = index & (half - 1)
            low = index < half
            pair0 = jnp.where(low, lane_gather(lows[0], lane), lane_gather(highs[0], lane))
            pair1 = jnp.where(low, lane_gather(lows[1], lane), lane_gather(highs[1], lane))
            reds.append((pair0 & 0xFFFF).astype(F32))
            greens.append((pair0 >> 16).astype(F32))
            blues.append((pair1 & 0xFFFF).astype(F32))
            clear.append(jnp.exp((pair1 >> 16).astype(F32) * optical_scale))
        ahead = [jnp.ones_like(clear[0])]
        for z in range(layers):
            ahead.append(ahead[-1] * clear[z])
        behind = jnp.ones_like(clear[0])
        for z in reversed(range(layers)):
            weight = jnp.where(near, ahead[z], behind) * ((1.0 - clear[z]) * (1.0 / UNIT))
            behind = behind * clear[z]
            shade_in[0, z, pl.ds(r0, block), :] = reds[z] * weight
            shade_in[1, z, pl.ds(r0, block), :] = greens[z] * weight
            shade_in[2, z, pl.ds(r0, block), :] = blues[z] * weight
        send[b, 3] = ahead[layers]
        return carry

    lax.fori_loop(0, count, lookup_block, 0, unroll=2 if count % 2 == 0 else 1)

    for _, arrives, copy in halos:
        pl.when(arrives)(copy.wait_recv)
    field[pl.ds(0, 2)] = layer_halo[0].astype(F32)
    field[pl.ds(layers + 2, 2)] = layer_halo[1].astype(F32)
    place = iota((32, cols), 0)
    outside = jnp.where(place == 2, -2, jnp.where(place == 3, -1, jnp.where(
        place == 16, cols, jnp.where(place == 17, cols + 1, -8))))
    band_e = stencil(outside - iota((32, cols), 1))
    grad_c[...] += matmul(edge_halo[...], band_e, ((0,), (0,))).reshape(layers, rows, cols)

    def shade_block(p):
        r0 = pl.multiple_of(p * block, block)
        f = [field[z, pl.ds(r0, block), :] for z in range(layers + 4)]
        colours = [jnp.zeros((block, cols), F32)] * 3
        for z in range(layers):
            gc = grad_c[z, pl.ds(r0, block), :]
            gr = grad_r[z, pl.ds(r0, block), :]
            gd = 8.0 * (f[z + 3] - f[z + 1]) - (f[z + 4] - f[z])
            dot = LIGHT_DIRECTION[0] * gc + LIGHT_DIRECTION[1] * gr + LIGHT_DIRECTION[2] * gd
            squared = gc * gc + gr * gr + gd * gd
            shading = AMBIENT + DIFFUSE * jnp.abs(dot) * lax.rsqrt(squared + 144.0)
            colours = [
                c + shade_in[i, z, pl.ds(r0, block), :] * shading for i, c in enumerate(colours)
            ]
        return colours

    def part_copy(k):
        p = partner(k)
        return remote(
            send.at[p], land.at[me], part_send.at[k], part_recv.at[k], {"depth": p})

    def send_block(k):
        p = partner(k)
        for c, colour in enumerate(shade_block(p)):
            send[p, c] = colour
        part_copy(k).start()

    if count <= 8:
        for k in reversed(range(1, count)):
            send_block(k)
    else:
        def step(i, carry):
            send_block(count - 1 - i)
            return carry

        lax.fori_loop(0, count - 1, step, 0)

    for c, colour in enumerate(shade_block(me)):
        land[me, c] = colour
    land[me, 3] = send[me, 3]

    for k in reversed(range(1, count)):
        part_copy(k).wait_recv()

    from_low = [jnp.zeros((block, cols), F32)] * 3
    from_high = from_low
    through = jnp.ones((block, cols), F32)
    for j in range(count):
        part_t = land[j, 3]
        through = through * part_t
        from_high = [land[j, c] + part_t * x for c, x in enumerate(from_high)]
    for j in reversed(range(count)):
        part_t = land[j, 3]
        from_low = [land[j, c] + part_t * x for c, x in enumerate(from_low)]
    for c in range(3):
        image_ref[c] = jnp.where(near, from_low[c], from_high[c])
    image_ref[3] = 1.0 - through

    for sends, _, copy in halos:
        pl.when(sends)(copy.wait_send)
    for k in range(1, count):
        part_copy(k).wait_send()


def on_device(density, bin_index, transfer, view_side):
    count, screens = lax.axis_size("depth"), lax.axis_size("screen")
    layers, rows, cols = density.shape
    block = rows // count
    vmem = pl.BlockSpec(memory_space=pltpu.VMEM)
    hbm = pl.BlockSpec(memory_space=pl.ANY)
    whole = (layers, rows, cols)
    return pl.pallas_call(
        functools.partial(render_kernel, count, screens),
        out_shape=jax.ShapeDtypeStruct((4, block, cols), F32),
        in_specs=[hbm, hbm, vmem, vmem],
        out_specs=vmem,
        scratch_shapes=[
            pltpu.VMEM(whole, BF16),
            pltpu.VMEM(whole, jnp.int32),
            pltpu.VMEM((2, 2, rows, cols), BF16),
            pltpu.VMEM((16, layers * rows), BF16),
            pltpu.VMEM((32, layers * rows), BF16),
            pltpu.VMEM((layers + 4, rows, cols), F32),
            pltpu.VMEM(whole, F32),
            pltpu.VMEM(whole, F32),
            pltpu.VMEM((3,) + whole, F32),
            pltpu.VMEM((count, 4, block, cols), F32),
            pltpu.VMEM((count, 4, block, cols), F32),
            pltpu.SemaphoreType.DMA((2,)),
            pltpu.SemaphoreType.DMA((4,)),
            pltpu.SemaphoreType.DMA((4,)),
            pltpu.SemaphoreType.DMA((count,)),
            pltpu.SemaphoreType.DMA((count,)),
        ],
        compiler_params=pltpu.CompilerParams(
            collective_id=0, has_side_effects=True, vmem_limit_bytes=40 * 2**20
        ),
        name="render",
    )(density, bin_index, transfer, view_side.reshape(1, cols))


def solution(mesh):
    placed = (P("depth", None, "screen"), P("depth", None, "screen"), P(), P("screen"))
    return jax.shard_map(
        on_device, mesh=mesh, in_specs=placed, out_specs=P(None, "depth", "screen"), check_vma=False
    )
```

```python
import functools

import jax
import jax.numpy as jnp
from jax import lax
from jax.experimental import pallas as pl
from jax.experimental.pallas import tpu as pltpu
from jax.sharding import PartitionSpec as P

LIGHT_DIRECTION = (0.36, 0.48, 0.8)
AMBIENT = 0.3
DIFFUSE = 0.7
OPTICAL = 4.0
UNIT = 4096
MESH = pl.DeviceIdType.MESH
F32 = jnp.float32
BF16 = jnp.bfloat16


def lane_gather(table, lanes):
    return lax.gather(
        table,
        lanes[..., None],
        lax.GatherDimensionNumbers(
            offset_dims=(),
            collapsed_slice_dims=(1,),
            start_index_map=(1,),
            operand_batching_dims=(0,),
            start_indices_batching_dims=(0,),
        ),
        slice_sizes=(1, 1),
        mode=lax.GatherScatterMode.PROMISE_IN_BOUNDS,
    )


def stencil(distance):
    one = jnp.where(distance == 1, 8.0, jnp.where(distance == -1, -8.0, 0.0))
    two = jnp.where(distance == 2, -1.0, jnp.where(distance == -2, 1.0, 0.0))
    return (one + two).astype(BF16)


def iota(shape, axis):
    return lax.broadcasted_iota(jnp.int32, shape, axis)


def matmul(a, b, dims=((1,), (0,))):
    return lax.dot_general(a, b, (dims, ((), ())), preferred_element_type=F32)


def render_kernel(
    count, screens,
    density_hbm, bins_hbm, table_hbm, side_hbm, image_ref,
    dens, bins, table_ref, side_ref, layer_halo, edge, edge_halo, field, grad_r, grad_c, shade_in,
    send, land,
    in_sem, halo_send, halo_recv, part_send, part_recv,
):
    layers, rows, cols = density_hbm.shape
    block = rows // count
    me = lax.axis_index("depth")
    col = lax.axis_index("screen")
    has_prev, has_next = me > 0, me < count - 1
    has_left, has_right = col > 0, col < screens - 1
    powers = count & (count - 1) == 0

    def partner(k):
        return me ^ k if powers else lax.rem(me + k, count)

    barrier = pltpu.get_barrier_semaphore()
    for k in range(1, count):
        pl.semaphore_signal(barrier, inc=1, device_id={"depth": partner(k)}, device_id_type=MESH)

    @pl.when(has_left)
    def _():
        pl.semaphore_signal(barrier, inc=1, device_id={"screen": col - 1}, device_id_type=MESH)

    @pl.when(has_right)
    def _():
        pl.semaphore_signal(barrier, inc=1, device_id={"screen": col + 1}, device_id_type=MESH)

    load_dens = pltpu.make_async_copy(density_hbm, dens, in_sem.at[0])
    load_bins = pltpu.make_async_copy(bins_hbm, bins, in_sem.at[1])
    load_table = pltpu.make_async_copy(table_hbm, table_ref, in_sem.at[2])
    load_side = pltpu.make_async_copy(side_hbm, side_ref, in_sem.at[3])
    load_dens.start()
    load_table.start()
    load_side.start()
    load_bins.start()

    zeros_layer = jnp.zeros((2, rows, cols), BF16)
    zeros_edge = jnp.zeros((16, layers * rows), BF16)

    @pl.when(jnp.logical_not(has_prev))
    def _():
        layer_halo[0] = zeros_layer

    @pl.when(jnp.logical_not(has_next))
    def _():
        layer_halo[1] = zeros_layer

    @pl.when(jnp.logical_not(has_left))
    def _():
        edge_halo[pl.ds(0, 16)] = zeros_edge

    @pl.when(jnp.logical_not(has_right))
    def _():
        edge_halo[pl.ds(16, 16)] = zeros_edge

    load_dens.wait()
    flat = dens[...].reshape(layers * rows, cols)
    slot = iota((16, cols), 0)
    wanted = jnp.where(slot < 2, slot, jnp.where(slot < 4, cols - 4 + slot, -1))
    pick = (iota((16, cols), 1) == wanted).astype(F32).astype(BF16)
    edge[...] = matmul(pick, flat, ((1,), (1,))).astype(BF16)

    greeted = count - 1 + has_left.astype(jnp.int32) + has_right.astype(jnp.int32)
    pl.semaphore_wait(barrier, greeted)

    def remote(src, dst, send_sem, recv_sem, target):
        return pltpu.make_async_remote_copy(
            src_ref=src, dst_ref=dst, send_sem=send_sem, recv_sem=recv_sem,
            device_id=target, device_id_type=MESH,
        )

    halos = (
        (has_next, has_prev, remote(
            density_hbm.at[pl.ds(layers - 2, 2)], layer_halo.at[0],
            halo_send.at[0], halo_recv.at[0], {"depth": me + 1})),
        (has_prev, has_next, remote(
            density_hbm.at[pl.ds(0, 2)], layer_halo.at[1],
            halo_send.at[1], halo_recv.at[1], {"depth": me - 1})),
        (has_right, has_left, remote(
            edge, edge_halo.at[pl.ds(0, 16)],
            halo_send.at[2], halo_recv.at[2], {"screen": col + 1})),
        (has_left, has_right, remote(
            edge, edge_halo.at[pl.ds(16, 16)],
            halo_send.at[3], halo_recv.at[3], {"screen": col - 1})),
    )
    for sends, _, copy in halos:
        pl.when(sends)(copy.start)

    band_c = stencil(iota((cols, cols), 0) - iota((cols, cols), 1))
    band_r = stencil(iota((rows, rows), 1) - iota((rows, rows), 0))
    grad_c[...] = matmul(flat, band_c).reshape(layers, rows, cols)
    for z in range(layers):
        grad_r[z] = matmul(band_r, dens[z])
    field[pl.ds(2, layers)] = dens[...].astype(F32)

    load_table.wait()
    load_side.wait()
    load_bins.wait()
    units = (table_ref[...].astype(F32) * UNIT).astype(jnp.int32)
    pairs = (units[0:1] | (units[1:2] << 16), units[2:3] | (units[3:4] << 16))
    half = units.shape[1] // 2
    lows = [jnp.broadcast_to(p[:, :half], (block, half)) for p in pairs]
    highs = [jnp.broadcast_to(p[:, half:], (block, half)) for p in pairs]
    near = jnp.broadcast_to(side_ref[...] == 0, (block, cols))
    optical_scale = -OPTICAL / (layers * count) / UNIT

    def lookup_block(b, carry):
        r0 = pl.multiple_of(b * block, block)
        clear, reds, greens, blues = [], [], [], []
        for z in range(layers):
            index = bins[z, pl.ds(r0, block), :]
            lane = index & (half - 1)
            low = index < half
            pair0 = jnp.where(low, lane_gather(lows[0], lane), lane_gather(highs[0], lane))
            pair1 = jnp.where(low, lane_gather(lows[1], lane), lane_gather(highs[1], lane))
            reds.append((pair0 & 0xFFFF).astype(F32))
            greens.append((pair0 >> 16).astype(F32))
            blues.append((pair1 & 0xFFFF).astype(F32))
            clear.append(jnp.exp((pair1 >> 16).astype(F32) * optical_scale))
        ahead = [jnp.ones_like(clear[0])]
        for z in range(layers):
            ahead.append(ahead[-1] * clear[z])
        behind = jnp.ones_like(clear[0])
        for z in reversed(range(layers)):
            weight = jnp.where(near, ahead[z], behind) * ((1.0 - clear[z]) * (1.0 / UNIT))
            behind = behind * clear[z]
            shade_in[0, z, pl.ds(r0, block), :] = reds[z] * weight
            shade_in[1, z, pl.ds(r0, block), :] = greens[z] * weight
            shade_in[2, z, pl.ds(r0, block), :] = blues[z] * weight
        send[b, 3] = ahead[layers]
        return carry

    lax.fori_loop(0, count, lookup_block, 0, unroll=2 if count % 2 == 0 else 1)

    for _, arrives, copy in halos:
        pl.when(arrives)(copy.wait_recv)
    field[pl.ds(0, 2)] = layer_halo[0].astype(F32)
    field[pl.ds(layers + 2, 2)] = layer_halo[1].astype(F32)
    place = iota((32, cols), 0)
    outside = jnp.where(place == 2, -2, jnp.where(place == 3, -1, jnp.where(
        place == 16, cols, jnp.where(place == 17, cols + 1, -8))))
    band_e = stencil(outside - iota((32, cols), 1))
    grad_c[...] += matmul(edge_halo[...], band_e, ((0,), (0,))).reshape(layers, rows, cols)

    def shade_block(p):
        r0 = pl.multiple_of(p * block, block)
        f = [field[z, pl.ds(r0, block), :] for z in range(layers + 4)]
        colours = [jnp.zeros((block, cols), F32)] * 3
        for z in range(layers):
            gc = grad_c[z, pl.ds(r0, block), :]
            gr = grad_r[z, pl.ds(r0, block), :]
            gd = 8.0 * (f[z + 3] - f[z + 1]) - (f[z + 4] - f[z])
            dot = LIGHT_DIRECTION[0] * gc + LIGHT_DIRECTION[1] * gr + LIGHT_DIRECTION[2] * gd
            squared = gc * gc + gr * gr + gd * gd
            shading = AMBIENT + DIFFUSE * jnp.abs(dot) * lax.rsqrt(squared + 144.0)
            colours = [
                c + shade_in[i, z, pl.ds(r0, block), :] * shading for i, c in enumerate(colours)
            ]
        return colours

    def part_copy(k):
        p = partner(k)
        return remote(
            send.at[p], land.at[me], part_send.at[k], part_recv.at[k], {"depth": p})

    def send_block(k):
        p = partner(k)
        for c, colour in enumerate(shade_block(p)):
            send[p, c] = colour
        part_copy(k).start()

    if count <= 8:
        for k in reversed(range(1, count)):
            send_block(k)
    else:
        def step(i, carry):
            send_block(count - 1 - i)
            return carry

        lax.fori_loop(0, count - 1, step, 0)

    for c, colour in enumerate(shade_block(me)):
        land[me, c] = colour
    land[me, 3] = send[me, 3]

    for k in reversed(range(1, count)):
        part_copy(k).wait_recv()

    from_low = [jnp.zeros((block, cols), F32)] * 3
    from_high = from_low
    through = jnp.ones((block, cols), F32)
    for j in range(count):
        part_t = land[j, 3]
        through = through * part_t
        from_high = [land[j, c] + part_t * x for c, x in enumerate(from_high)]
    for j in reversed(range(count)):
        part_t = land[j, 3]
        from_low = [land[j, c] + part_t * x for c, x in enumerate(from_low)]
    for c in range(3):
        image_ref[c] = jnp.where(near, from_low[c], from_high[c])
    image_ref[3] = 1.0 - through

    for sends, _, copy in halos:
        pl.when(sends)(copy.wait_send)
    for k in range(1, count):
        part_copy(k).wait_send()


def on_device(density, bin_index, transfer, view_side):
    count, screens = lax.axis_size("depth"), lax.axis_size("screen")
    layers, rows, cols = density.shape
    block = rows // count
    vmem = pl.BlockSpec(memory_space=pltpu.VMEM)
    hbm = pl.BlockSpec(memory_space=pltpu.HBM)
    whole = (layers, rows, cols)
    return pl.pallas_call(
        functools.partial(render_kernel, count, screens),
        out_shape=jax.ShapeDtypeStruct((4, block, cols), F32),
        in_specs=[hbm] * 4,
        out_specs=vmem,
        scratch_shapes=[
            pltpu.VMEM(whole, BF16),
            pltpu.VMEM(whole, jnp.int32),
            pltpu.VMEM(transfer.shape, BF16),
            pltpu.VMEM((1, cols), jnp.int32),
            pltpu.VMEM((2, 2, rows, cols), BF16),
            pltpu.VMEM((16, layers * rows), BF16),
            pltpu.VMEM((32, layers * rows), BF16),
            pltpu.VMEM((layers + 4, rows, cols), F32),
            pltpu.VMEM(whole, F32),
            pltpu.VMEM(whole, F32),
            pltpu.VMEM((3,) + whole, F32),
            pltpu.VMEM((count, 4, block, cols), F32),
            pltpu.VMEM((count, 4, block, cols), F32),
            pltpu.SemaphoreType.DMA((4,)),
            pltpu.SemaphoreType.DMA((4,)),
            pltpu.SemaphoreType.DMA((4,)),
            pltpu.SemaphoreType.DMA((count,)),
            pltpu.SemaphoreType.DMA((count,)),
        ],
        compiler_params=pltpu.CompilerParams(
            collective_id=0, has_side_effects=True, vmem_limit_bytes=64 * 2**20
        ),
        name="render",
    )(density, bin_index, transfer, view_side.reshape(1, cols))


def solution(mesh):
    placed = (P("depth", None, "screen"), P("depth", None, "screen"), P(), P("screen"))
    return jax.shard_map(
        on_device, mesh=mesh, in_specs=placed, out_specs=P(None, "depth", "screen"), check_vma=False
    )
```

```python
import functools

import jax
import jax.numpy as jnp
from jax import lax
from jax.experimental import pallas as pl
from jax.experimental.pallas import tpu as pltpu
from jax.sharding import PartitionSpec as P

LIGHT_DIRECTION = (0.36, 0.48, 0.8)
AMBIENT = 0.3
DIFFUSE = 0.7
OPTICAL = 4.0
UNIT = 4096
LEVELS = 65534
MESH = pl.DeviceIdType.MESH
F32 = jnp.float32
BF16 = jnp.bfloat16


def lane_gather(table, lanes):
    return lax.gather(
        table,
        lanes[..., None],
        lax.GatherDimensionNumbers(
            offset_dims=(),
            collapsed_slice_dims=(1,),
            start_index_map=(1,),
            operand_batching_dims=(0,),
            start_indices_batching_dims=(0,),
        ),
        slice_sizes=(1, 1),
        mode=lax.GatherScatterMode.PROMISE_IN_BOUNDS,
    )


def stencil(distance):
    one = jnp.where(distance == 1, 8.0, jnp.where(distance == -1, -8.0, 0.0))
    two = jnp.where(distance == 2, -1.0, jnp.where(distance == -2, 1.0, 0.0))
    return (one + two).astype(BF16)


def iota(shape, axis):
    return lax.broadcasted_iota(jnp.int32, shape, axis)


def matmul(a, b, dims=((1,), (0,))):
    return lax.dot_general(a, b, (dims, ((), ())), preferred_element_type=F32)


def render_kernel(
    count, screens,
    density_hbm, bins_hbm, table_hbm, side_hbm, image_ref,
    dens, bins, table_ref, side_ref, layer_halo, edge, edge_halo, field, grad_r, grad_c, shade_in,
    extinct, send, land,
    in_sem, halo_send, halo_recv, part_send, part_recv,
):
    layers, rows, cols = density_hbm.shape
    block = rows // count
    me = lax.axis_index("depth")
    col = lax.axis_index("screen")
    has_prev, has_next = me > 0, me < count - 1
    has_left, has_right = col > 0, col < screens - 1
    powers = count & (count - 1) == 0

    def partner(k):
        return me ^ k if powers else lax.rem(me + k, count)

    barrier = pltpu.get_barrier_semaphore()
    for k in range(1, count):
        pl.semaphore_signal(barrier, inc=1, device_id={"depth": partner(k)}, device_id_type=MESH)

    @pl.when(has_left)
    def _():
        pl.semaphore_signal(barrier, inc=1, device_id={"screen": col - 1}, device_id_type=MESH)

    @pl.when(has_right)
    def _():
        pl.semaphore_signal(barrier, inc=1, device_id={"screen": col + 1}, device_id_type=MESH)

    load_dens = pltpu.make_async_copy(density_hbm, dens, in_sem.at[0])
    load_bins = pltpu.make_async_copy(bins_hbm, bins, in_sem.at[1])
    load_table = pltpu.make_async_copy(table_hbm, table_ref, in_sem.at[2])
    load_side = pltpu.make_async_copy(side_hbm, side_ref, in_sem.at[3])
    load_dens.start()
    load_table.start()
    load_side.start()
    load_bins.start()

    zeros_layer = jnp.zeros((2, rows, cols), BF16)
    zeros_edge = jnp.zeros((16, layers * rows), BF16)

    @pl.when(jnp.logical_not(has_prev))
    def _():
        layer_halo[0] = zeros_layer

    @pl.when(jnp.logical_not(has_next))
    def _():
        layer_halo[1] = zeros_layer

    @pl.when(jnp.logical_not(has_left))
    def _():
        edge_halo[pl.ds(0, 16)] = zeros_edge

    @pl.when(jnp.logical_not(has_right))
    def _():
        edge_halo[pl.ds(16, 16)] = zeros_edge

    load_dens.wait()
    flat = dens[...].reshape(layers * rows, cols)
    slot = iota((16, cols), 0)
    wanted = jnp.where(slot < 2, slot, jnp.where(slot < 4, cols - 4 + slot, -1))
    pick = (iota((16, cols), 1) == wanted).astype(F32).astype(BF16)
    edge[...] = matmul(pick, flat, ((1,), (1,))).astype(BF16)

    greeted = count - 1 + has_left.astype(jnp.int32) + has_right.astype(jnp.int32)
    pl.semaphore_wait(barrier, greeted)

    def remote(src, dst, send_sem, recv_sem, target):
        return pltpu.make_async_remote_copy(
            src_ref=src, dst_ref=dst, send_sem=send_sem, recv_sem=recv_sem,
            device_id=target, device_id_type=MESH,
        )

    halos = (
        (has_next, has_prev, remote(
            density_hbm.at[pl.ds(layers - 2, 2)], layer_halo.at[0],
            halo_send.at[0], halo_recv.at[0], {"depth": me + 1})),
        (has_prev, has_next, remote(
            density_hbm.at[pl.ds(0, 2)], layer_halo.at[1],
            halo_send.at[1], halo_recv.at[1], {"depth": me - 1})),
        (has_right, has_left, remote(
            edge, edge_halo.at[pl.ds(0, 16)],
            halo_send.at[2], halo_recv.at[2], {"screen": col + 1})),
        (has_left, has_right, remote(
            edge, edge_halo.at[pl.ds(16, 16)],
            halo_send.at[3], halo_recv.at[3], {"screen": col - 1})),
    )
    for sends, _, copy in halos:
        pl.when(sends)(copy.start)

    band_c = stencil(iota((cols, cols), 0) - iota((cols, cols), 1))
    band_r = stencil(iota((rows, rows), 1) - iota((rows, rows), 0))
    grad_c[...] = matmul(flat, band_c).reshape(layers, rows, cols)
    for z in range(layers):
        grad_r[z] = matmul(band_r, dens[z])
    field[pl.ds(2, layers)] = dens[...].astype(F32)

    load_table.wait()
    load_side.wait()
    load_bins.wait()
    units = (table_ref[...].astype(F32) * UNIT).astype(jnp.int32)
    pairs = (units[0:1] | (units[1:2] << 16), units[2:3] | (units[3:4] << 16))
    half = units.shape[1] // 2
    lows = [jnp.broadcast_to(p[:, :half], (block, half)) for p in pairs]
    highs = [jnp.broadcast_to(p[:, half:], (block, half)) for p in pairs]
    near = jnp.broadcast_to(side_ref[...] == 0, (block, cols))
    optical_scale = -OPTICAL / (layers * count) / UNIT

    def lookup_block(b, carry):
        r0 = pl.multiple_of(b * block, block)
        clear, reds, greens, blues = [], [], [], []
        total = jnp.zeros((block, cols), F32)
        for z in range(layers):
            index = bins[z, pl.ds(r0, block), :]
            lane = index & (half - 1)
            low = index < half
            pair0 = jnp.where(low, lane_gather(lows[0], lane), lane_gather(highs[0], lane))
            pair1 = jnp.where(low, lane_gather(lows[1], lane), lane_gather(highs[1], lane))
            reds.append((pair0 & 0xFFFF).astype(F32))
            greens.append((pair0 >> 16).astype(F32))
            blues.append((pair1 & 0xFFFF).astype(F32))
            extinction = (pair1 >> 16).astype(F32)
            total = total + extinction
            clear.append(jnp.exp(extinction * optical_scale))
        ahead = [jnp.ones_like(clear[0])]
        for z in range(layers - 1):
            ahead.append(ahead[-1] * clear[z])
        behind = jnp.ones_like(clear[0])
        for z in reversed(range(layers)):
            weight = jnp.where(near, ahead[z], behind) * ((1.0 - clear[z]) * (1.0 / UNIT))
            behind = behind * clear[z]
            shade_in[0, z, pl.ds(r0, block), :] = reds[z] * weight
            shade_in[1, z, pl.ds(r0, block), :] = greens[z] * weight
            shade_in[2, z, pl.ds(r0, block), :] = blues[z] * weight
        extinct[pl.ds(r0, block), :] = total
        return carry

    lax.fori_loop(0, count, lookup_block, 0, unroll=2 if count % 2 == 0 else 1)

    for _, arrives, copy in halos:
        pl.when(arrives)(copy.wait_recv)
    field[pl.ds(0, 2)] = layer_halo[0].astype(F32)
    field[pl.ds(layers + 2, 2)] = layer_halo[1].astype(F32)
    place = iota((32, cols), 0)
    outside = jnp.where(place == 2, -2, jnp.where(place == 3, -1, jnp.where(
        place == 16, cols, jnp.where(place == 17, cols + 1, -8))))
    band_e = stencil(outside - iota((32, cols), 1))
    grad_c[...] += matmul(edge_halo[...], band_e, ((0,), (0,))).reshape(layers, rows, cols)

    def shade_block(p):
        r0 = pl.multiple_of(p * block, block)
        f = [field[z, pl.ds(r0, block), :] for z in range(layers + 4)]
        colours = [jnp.zeros((block, cols), F32)] * 3
        for z in range(layers):
            gc = grad_c[z, pl.ds(r0, block), :]
            gr = grad_r[z, pl.ds(r0, block), :]
            gd = 8.0 * (f[z + 3] - f[z + 1]) - (f[z + 4] - f[z])
            dot = LIGHT_DIRECTION[0] * gc + LIGHT_DIRECTION[1] * gr + LIGHT_DIRECTION[2] * gd
            squared = gc * gc + gr * gr + gd * gd
            shading = AMBIENT + DIFFUSE * jnp.abs(dot) * lax.rsqrt(squared + 144.0)
            colours = [
                c + shade_in[i, z, pl.ds(r0, block), :] * shading for i, c in enumerate(colours)
            ]
        total = extinct[pl.ds(r0, block), :]
        spread = LEVELS / (1.0 - jnp.exp(total * optical_scale))
        codes = [jnp.minimum(c * spread, LEVELS) - (LEVELS // 2 - 0.5) for c in colours]
        codes = jnp.concatenate(codes + [total - layers * UNIT // 2], axis=0)
        return jnp.floor(codes).astype(jnp.int32).astype(jnp.int16)

    def part_copy(k):
        p = partner(k)
        return remote(
            send.at[p], land.at[me], part_send.at[k], part_recv.at[k], {"depth": p})

    def send_block(k):
        p = partner(k)
        send[p] = shade_block(p)
        part_copy(k).start()

    if count <= 8:
        for k in reversed(range(1, count)):
            send_block(k)
    else:
        def step(i, carry):
            send_block(count - 1 - i)
            return carry

        lax.fori_loop(0, count - 1, step, 0)

    land[me] = shade_block(me)

    for k in reversed(range(1, count)):
        part_copy(k).wait_recv()

    parts = []
    for j in range(count):
        codes = land[j].astype(jnp.int32).astype(F32)
        total = codes[3 * block:] + layers * UNIT // 2
        part_t = jnp.exp(total * optical_scale)
        spread = (1.0 - part_t) * (1.0 / LEVELS)
        parts.append([
            (codes[c * block:(c + 1) * block] + LEVELS // 2) * spread for c in range(3)
        ] + [part_t])
    from_low = [jnp.zeros((block, cols), F32)] * 3
    from_high = from_low
    through = jnp.ones((block, cols), F32)
    for part in parts:
        through = through * part[3]
        from_high = [part[c] + part[3] * x for c, x in enumerate(from_high)]
    for part in reversed(parts):
        from_low = [part[c] + part[3] * x for c, x in enumerate(from_low)]
    for c in range(3):
        image_ref[c] = jnp.where(near, from_low[c], from_high[c])
    image_ref[3] = 1.0 - through

    for sends, _, copy in halos:
        pl.when(sends)(copy.wait_send)
    for k in range(1, count):
        part_copy(k).wait_send()


def on_device(density, bin_index, transfer, view_side):
    count, screens = lax.axis_size("depth"), lax.axis_size("screen")
    layers, rows, cols = density.shape
    block = rows // count
    vmem = pl.BlockSpec(memory_space=pltpu.VMEM)
    hbm = pl.BlockSpec(memory_space=pltpu.HBM)
    whole = (layers, rows, cols)
    return pl.pallas_call(
        functools.partial(render_kernel, count, screens),
        out_shape=jax.ShapeDtypeStruct((4, block, cols), F32),
        in_specs=[hbm] * 4,
        out_specs=vmem,
        scratch_shapes=[
            pltpu.VMEM(whole, BF16),
            pltpu.VMEM(whole, jnp.int32),
            pltpu.VMEM(transfer.shape, BF16),
            pltpu.VMEM((1, cols), jnp.int32),
            pltpu.VMEM((2, 2, rows, cols), BF16),
            pltpu.VMEM((16, layers * rows), BF16),
            pltpu.VMEM((32, layers * rows), BF16),
            pltpu.VMEM((layers + 4, rows, cols), F32),
            pltpu.VMEM(whole, F32),
            pltpu.VMEM(whole, F32),
            pltpu.VMEM((3,) + whole, F32),
            pltpu.VMEM((rows, cols), F32),
            pltpu.VMEM((count, 4 * block, cols), jnp.int16),
            pltpu.VMEM((count, 4 * block, cols), jnp.int16),
            pltpu.SemaphoreType.DMA((4,)),
            pltpu.SemaphoreType.DMA((4,)),
            pltpu.SemaphoreType.DMA((4,)),
            pltpu.SemaphoreType.DMA((count,)),
            pltpu.SemaphoreType.DMA((count,)),
        ],
        compiler_params=pltpu.CompilerParams(
            collective_id=0, has_side_effects=True, vmem_limit_bytes=64 * 2**20
        ),
        name="render",
    )(density, bin_index, transfer, view_side.reshape(1, cols))


def solution(mesh):
    placed = (P("depth", None, "screen"), P("depth", None, "screen"), P(), P("screen"))
    return jax.shard_map(
        on_device, mesh=mesh, in_specs=placed, out_specs=P(None, "depth", "screen"), check_vma=False
    )
```
